32 devices in a mesh: dp: 4 (over y, x), space: 8 (over z, core).
Axes of the slice: x: 2, y: 2, z: 4, core: 2. Of those that a mesh axis runs over, the one named last changes fastest.
Arguments:
- image: bfloat16 [4, 64, 10240], P('dp', 'space'), may hold values from -6 to 6
- cotangent: bfloat16 [4, 32, 5120], P('dp', 'space'), may hold values from -6 to 6
- weight: float32 [1440, 160], P('dp'), may hold values from -0.15625 to 0.15625
- moment_one: float32 [1440, 160], P('dp'), may hold values from -0.25 to 0.25
- moment_two: float32 [1440, 160], P('dp'), may hold values from 6.1035156e-05 to 0.0009765625
Outputs:
- output: bfloat16 [4, 32, 5120], P('dp', 'space')
- grad_image: bfloat16 [4, 64, 10240], P('dp', 'space')
- new_weight: float32 [1440, 160], P('dp')
- new_moment_one: float32 [1440, 160], P('dp')
- new_moment_two: float32 [1440, 160], P('dp')
The draws below stay inside these ranges and needn't reach their ends.
All inputs are finite; a program needn't handle non-finite values.
Results may differ from the reference program's by a relative error of at most 0.0049.
Values may be sent and summed in bfloat16 or wider, within the bound.
A program may use at most 64 MiB of HBM per device.

```python
import math
import jax
import jax.numpy as jnp
from jax import lax

C = 160
W = 64
BATCH = 4
H = 64
OH = 32
OW = 32
KROWS = 1440
COUNT = 4096


def block_levels(rng, shape, pieces, low, top_value):
    loudness = 1.0
    for position, blocks in pieces:
        heights = jax.random.uniform(jax.random.fold_in(jax.random.fold_in(rng, 6), position), (blocks,), jnp.float32, low / len(pieces), top_value / len(pieces))
        loudness = loudness * jnp.repeat(jnp.exp(heights), shape[position] // blocks).reshape((-1,) + (1,) * (len(shape) - 1 - position))
    return loudness


def centred(stream_key, dims, deviation, limit, pieces=(), kind=jnp.bfloat16):
    values = deviation * jax.random.normal(stream_key, dims, jnp.float32)
    if pieces:
        values = values * block_levels(stream_key, dims, pieces, -0.22, 0.18)
    return jnp.clip(values, -limit, limit).astype(kind)


def setup_inputs(seed: int = 0) -> dict:
    key_of = jax.random.split(jax.random.key(seed), 6)
    image = centred(key_of[0], (BATCH, H, W * C), 1.0, 6.0, ((0, 4), (1, 8)))
    cotangent = centred(key_of[1], (BATCH, OH, OW * C), 1.0, 6.0, ((0, 4), (1, 8)))
    weight = centred(key_of[2], (KROWS, C), KROWS ** -0.5, 0.15625, ((0, 4),), jnp.float32)
    moment_one = centred(key_of[3], (KROWS, C), (COUNT ** -0.5), 0.25, ((0, 4),), jnp.float32)
    moment_two = jnp.clip(jnp.exp(math.log(0.0009765625) - 2.7725887 * jax.random.uniform(key_of[4], (KROWS, C), jnp.float32) ** block_levels(key_of[4], (KROWS, C), ((0, 4),), -0.2, 0.2)), 6.103515625e-05, 0.0009765625)
    return dict(image=image, cotangent=cotangent, weight=weight, moment_one=moment_one, moment_two=moment_two)


def convolve(sample, kernel):
    return lax.conv_general_dilated(sample[None], kernel, (2, 2), ((1, 1), (1, 1)), dimension_numbers=('NHWC', 'HWIO', 'NHWC'), precision=lax.Precision.HIGHEST)[0]

def reference(image, cotangent, weight, moment_one, moment_two):
    kernel = weight.astype(jnp.bfloat16).astype(jnp.float32).reshape(3, 3, C, C)
    image_four = image.reshape(BATCH, H, W, C)
    cotan_four = cotangent.reshape(BATCH, OH, OW, C)

    def per_sample(carried, inputs):
        sample_in, sample_cot = inputs
        forward, pullback = jax.vjp(convolve, sample_in.astype(jnp.float32), kernel)
        grad_in, grad_kernel = pullback(sample_cot.astype(jnp.float32))
        return (carried + grad_kernel, (forward.astype(jnp.bfloat16), grad_in.astype(jnp.bfloat16)))
    summed, (output, grad_image) = lax.scan(per_sample, jnp.zeros((3, 3, C, C), jnp.float32), (image_four, cotan_four))
    gradient = summed.reshape(KROWS, C) / COUNT
    new_moment_one = 0.9 * moment_one + 0.1 * gradient
    new_moment_two = 0.999 * moment_two + 0.001 * gradient * gradient
    first_hat = new_moment_one / (1.0 - 0.9 ** 10)
    second_hat = new_moment_two / (1.0 - 0.999 ** 10)
    new_weight = weight - 0.01 * (first_hat / (jnp.sqrt(second_hat) + 1e-08) + 0.01 * weight)
    output = output.reshape(BATCH, OH, OW * C)
    grad_image = grad_image.reshape(BATCH, H, W * C)
    return (output, grad_image, new_weight, new_moment_one, new_moment_two)
```

```python
import functools

import jax
import jax.numpy as jnp
from jax import lax
from jax.experimental import pallas as pl
from jax.experimental.pallas import tpu as pltpu
from jax.sharding import PartitionSpec as P

MESH = pl.DeviceIdType.MESH
F32 = jnp.float32
BF16 = jnp.bfloat16

beta_one = 0.9
beta_two = 0.999
learn_rate = 0.01
decay_rate = 0.01
epsilon = 1e-08
adam_step = 10


def up(value, unit):
    return -(-value // unit) * unit


def kernel(
    n_dp, n_space, count,
    image, cotangent, weight, moment_one, moment_two,
    out, grad_image, new_weight, new_one, new_two,
    even, odd, cot, cot_next, img_edge_out, img_edge_in, cot_edge_out, cot_edge_in,
    wt, taps, part, mate_out, mate_in, own, dp_out, dp_in, shares, z_out, z_in, final, total,
    edge_send, edge_recv, w_send, w_recv, wm_send, wm_recv, m_send, m_recv,
    d_send, d_recv, z_send, z_recv, f_send, f_recv,
):
    C = weight.shape[1]
    half = C // 2
    rest = C - 128
    shard = weight.shape[0]
    wide = wt.shape[-1]
    cols = out.shape[2] // C
    out_rows = out.shape[1]
    rows = image.shape[1]
    positions = cols * out_rows
    nz = n_space // 2
    sub = wide // nz
    dp = lax.axis_index("dp")
    space = lax.axis_index("space")
    core = lax.rem(space, 2)
    zi = lax.div(space, 2)
    mate = space + 1 - 2 * core

    barrier = pltpu.get_barrier_semaphore()
    for k in range(1, n_dp):
        pl.semaphore_signal(barrier, inc=1, device_id=(lax.rem(dp + k, n_dp), space), device_id_type=MESH)
    for k in range(1, n_space):
        pl.semaphore_signal(barrier, inc=1, device_id=(dp, lax.rem(space + k, n_space)), device_id_type=MESH)

    def remote(src, dst, send, recv, to_dp, to_space):
        return pltpu.make_async_remote_copy(
            src_ref=src, dst_ref=dst, send_sem=send, recv_sem=recv,
            device_id=(to_dp, to_space), device_id_type=MESH)

    zeros_e = jnp.zeros(even.shape[1:], F32)
    even[1] = zeros_e
    odd[1] = zeros_e
    odd[0, 0:16, :] = jnp.zeros((16, 128), F32)
    cot[1] = jnp.zeros(cot.shape[1:], F32)
    cot[0, pl.ds(positions, 8), :] = jnp.zeros((8, 128), F32)
    cot_next[0, pl.ds(positions, 8), :] = jnp.zeros((8, 128), F32)
    cot_next[1, pl.ds(positions, 8), :] = jnp.zeros((8, 128), F32)

    group = 4 * C

    def split_cot(g, carry):
        v = cotangent[0, :, pl.ds(pl.multiple_of(g * group, 128), group)].astype(F32)
        pieces = [v[:, k * C : (k + 1) * C] for k in range(4)]
        for k in range(0, 4, 2):
            both = jnp.concatenate([pieces[k], pieces[k + 1]], axis=0)
            at = pl.multiple_of((4 * g + k) * out_rows, 8)
            cot[0, pl.ds(at, 8), :] = both[:, :128]
            cot[1, pl.ds(at, 8), 0:rest] = both[:, 128:]
        return carry

    lax.fori_loop(0, cols // 4, split_cot, 0)

    def split_image(g, carry):
        v = image[0, :, pl.ds(pl.multiple_of(g * group, 128), group)].astype(F32)
        for k in range(4):
            piece = v[:, k * C : (k + 1) * C]
            ref = odd if k % 2 else even
            at = pl.multiple_of((2 * g + k // 2) * rows + 16, 8)
            ref[0, pl.ds(at, rows), :] = piece[:, :128]
            ref[1, pl.ds(at, rows), 0:rest] = piece[:, 128:]
        return carry

    lax.fori_loop(0, cols // 2, split_image, 0)

    def strided(ref, start, size, stride):
        at = pl.ds(start, size, stride=stride)
        return jnp.concatenate([ref[0, at, :], ref[1, at, :]], axis=1)[:, :C]

    img_edge_out[0:cols] = strided(even, 16 + rows - 1, cols, rows).astype(BF16)
    img_edge_out[cols : 2 * cols] = strided(odd, 16 + rows - 1, cols, rows).astype(BF16)
    cot_edge_out[...] = strided(cot, 0, cols, out_rows).astype(BF16)

    eye = (lax.broadcasted_iota(jnp.int32, (C, C), 0) == lax.broadcasted_iota(jnp.int32, (C, C), 1))
    eye = eye.astype(F32).astype(BF16)
    mine = lax.dot_general(eye, weight[...].astype(BF16), (((1,), (1,)), ((), ())),
                           preferred_element_type=F32).astype(BF16)
    wt[dp, 0, :, 0:shard] = mine[:half]
    wt[dp, 1, :, 0:shard] = mine[half:]

    pl.semaphore_wait(barrier, n_dp + n_space - 2)

    img_copy = remote(img_edge_out, img_edge_in, edge_send.at[0], edge_recv.at[0], dp, lax.rem(space + 1, n_space))
    cot_copy = remote(cot_edge_out, cot_edge_in, edge_send.at[1], edge_recv.at[1], dp, lax.rem(space + n_space - 1, n_space))

    img_copy.start()
    cot_copy.start()

    def w_copy(k):
        return remote(wt.at[dp, core], wt.at[dp, core], w_send.at[k], w_recv.at[k], lax.rem(dp + k, n_dp), space)

    for k in range(1, n_dp):
        w_copy(k).start()

    whole_cot = strided(cot, 0, positions, 1)
    cot_t = whole_cot.T.astype(BF16)
    first, second = cot_t[:half], cot_t[half:]
    lower = core == 0
    mate_rows = jnp.where(lower, second.astype(F32), first.astype(F32)).astype(BF16)
    own_rows = jnp.where(lower, first.astype(F32), second.astype(F32)).astype(BF16)

    def patch(r, s):
        ref = even if s == 1 else odd
        start = 16 + r - 1 - (rows if s == 0 else 0)
        return strided(ref, start, positions, 2).astype(BF16)

    def place(ref, tap, value, by_shard):
        lo = tap * C
        end = lo + C
        while lo < end:
            d = lo // shard
            stop = min(end, (d + 1) * shard)
            ref[d, :, lo - d * shard : stop - d * shard] = value[:, lo - tap * C : stop - tap * C]
            lo = stop

    for d in range(n_dp):
        if wide > shard:
            pad = jnp.zeros((half, wide - shard), F32)
            own[d, :, shard:wide] = pad
            part[d, :, shard:wide] = pad

    def grads(r):
        for s in range(3):
            p = patch(r, s)
            taps[3 * r + s] = p
            place(part, 3 * r + s, jnp.dot(mate_rows, p, preferred_element_type=F32), True)

    grads(1)
    grads(2)
    img_copy.wait()

    @pl.when(space == 0)
    def _():
        img_edge_in[...] = jnp.zeros(img_edge_in.shape, BF16)

    for base, ref in ((0, even), (cols, odd)):
        edge = img_edge_in[base : base + cols].astype(F32)
        at = pl.ds(15, cols, stride=rows)
        ref[0, at, :] = edge[:, :128]
        ref[1, at, :] = jnp.concatenate([edge[:, 128:], jnp.zeros((cols, 256 - C), F32)], axis=1)
    grads(0)
    mate_out[...] = part[...].astype(BF16)
    mate_copy = remote(mate_out, mate_in, m_send.at[0], m_recv.at[0], dp, mate)
    mate_copy.start()

    def wm_copy(k):
        src = lax.rem(dp + n_dp - k, n_dp)
        return remote(wt.at[src, core], wt.at[src, core], wm_send.at[k], wm_recv.at[k], dp, mate)

    for k in range(1, n_dp):
        w_copy(k).wait()
        wm_copy(k).start()

    for t in range(9):
        place(own, t, jnp.dot(own_rows, taps[t], preferred_element_type=F32), True)

    mate_copy.wait()
    own[...] = own[...] + mate_in[...].astype(F32)

    dp_out[...] = own[...].astype(BF16)

    def d_copy(k):
        to = lax.rem(dp + k, n_dp)
        return remote(dp_out.at[to], dp_in.at[k], d_send.at[k], d_recv.at[k], to, space)

    for k in range(1, n_dp):
        d_copy(k).start()

    for k in range(1, n_dp):
        wm_copy(k).wait()

    def tap_t(t):
        lo = t * C
        end = lo + C
        pieces = []
        while lo < end:
            d = lo // shard
            stop = min(end, (d + 1) * shard)
            at = slice(lo - d * shard, stop - d * shard)
            pieces.append(jnp.concatenate([wt[d, 0, :, at], wt[d, 1, :, at]], axis=0).astype(F32))
            lo = stop
        value = pieces[0] if len(pieces) == 1 else jnp.concatenate(pieces, axis=1)
        return value.astype(BF16)

    kern = [tap_t(t) for t in range(9)]
    acc = jnp.zeros((positions, C), F32)
    for t in range(9):
        acc = acc + lax.dot_general(taps[t], kern[t], (((1,), (1,)), ((), ())), preferred_element_type=F32)
    total_shape = total.shape

    def keep(ref, at, value):
        ref[0, at, :] = value[:, :128]
        ref[1, at, :] = jnp.concatenate([value[:, 128:], jnp.zeros((value.shape[0], 256 - C), F32)], axis=1)

    keep(even, pl.ds(0, positions), acc)

    def join_out(g, carry):
        pieces = []
        for k in range(0, 4, 2):
            at = pl.multiple_of((4 * g + k) * out_rows, 8)
            v = jnp.concatenate([even[0, pl.ds(at, 8), :], even[1, pl.ds(at, 8), 0:rest]], axis=1)
            pieces += [v[:out_rows], v[out_rows:]]
        out[0, :, pl.ds(pl.multiple_of(g * group, 128), group)] = jnp.concatenate(pieces, axis=1).astype(BF16)
        return carry

    lax.fori_loop(0, cols // 4, join_out, 0)

    cot_copy.wait()

    @pl.when(space == n_space - 1)
    def _():
        cot_edge_in[...] = jnp.zeros(cot_edge_in.shape, BF16)

    for h in range(2):
        cot_next[h, pl.ds(0, positions), :] = cot[h, pl.ds(1, positions), :]
    edge = cot_edge_in[...].astype(F32)
    at = pl.ds(out_rows - 1, cols, stride=out_rows)
    keep(cot_next, at, edge)
    here = whole_cot.astype(BF16)
    right = strided(cot, out_rows, positions, 1).astype(BF16)
    below = strided(cot_next, 0, positions, 1).astype(BF16)
    both = strided(cot_next, out_rows, positions, 1).astype(BF16)

    def back(c, r, s):
        return jnp.dot(c, kern[3 * r + s], preferred_element_type=F32)

    keep(even, pl.ds(0, positions, stride=2), back(here, 1, 1))
    keep(even, pl.ds(1, positions, stride=2), back(here, 2, 1) + back(below, 0, 1))
    keep(odd, pl.ds(0, positions, stride=2), back(here, 1, 2) + back(right, 1, 0))
    keep(odd, pl.ds(1, positions, stride=2),
         back(here, 2, 2) + back(right, 2, 0) + back(below, 0, 2) + back(both, 0, 0))

    def join_grad(g, carry):
        pieces = []
        for k in range(4):
            ref = odd if k % 2 else even
            at = pl.multiple_of((2 * g + k // 2) * rows, 8)
            pieces.append(jnp.concatenate([ref[0, pl.ds(at, rows), :], ref[1, pl.ds(at, rows), 0:rest]], axis=1))
        grad_image[0, :, pl.ds(pl.multiple_of(g * group, 128), group)] = jnp.concatenate(pieces, axis=1).astype(BF16)
        return carry

    lax.fori_loop(0, cols // 2, join_grad, 0)

    summed = own[dp]
    for k in range(1, n_dp):
        d_copy(k).wait()
        summed = summed + dp_in[k].astype(F32)
    for z in range(nz):
        piece = summed[:, z * sub : (z + 1) * sub]
        if sub < 128:
            piece = jnp.concatenate([piece, jnp.zeros((half, 128 - sub), F32)], axis=1)
        shares[z] = piece
        z_out[z] = piece.astype(BF16)

    def z_copy(k):
        to = lax.rem(zi + k, nz)
        return remote(z_out.at[to], z_in.at[k], z_send.at[k], z_recv.at[k], dp, 2 * to + core)

    for k in range(1, nz):
        z_copy(k).start()
    summed = shares[zi]
    for k in range(1, nz):
        z_copy(k).wait()
        summed = summed + z_in[k].astype(F32)

    final[space] = summed.astype(BF16)

    def f_copy(k):
        return remote(final.at[space], final.at[space], f_send.at[k], f_recv.at[k], dp, lax.rem(space + k, n_space))

    for k in range(1, n_space):
        f_copy(k).start()
    for k in range(1, n_space):
        f_copy(k).wait()
    for z in range(nz):
        for c in range(2):
            total[c * half : (c + 1) * half, z * sub : (z + 1) * sub] = final[2 * z + c].astype(F32)[:, :sub]
    gradient = total[...].T[:shard, :C] / float(count)

    one = beta_one * moment_one[...] + (1.0 - beta_one) * gradient
    two = beta_two * moment_two[...] + (1.0 - beta_two) * gradient * gradient
    first_hat = one / (1.0 - beta_one**adam_step)
    second_hat = two / (1.0 - beta_two**adam_step)
    old = weight[...]
    new_one[...] = one
    new_two[...] = two
    new_weight[...] = old - learn_rate * (first_hat / (jnp.sqrt(second_hat) + epsilon) + decay_rate * old)


def body(n_dp, n_space, image, cotangent, weight, moment_one, moment_two):
    shard, C = weight.shape
    half = C // 2
    wide = up(shard, 128)
    rows = image.shape[1]
    out_rows = cotangent.shape[1]
    cols = cotangent.shape[2] // C
    positions = out_rows * cols
    nz = n_space // 2
    count = positions * n_dp * n_space
    vmem = pltpu.VMEM
    dma = pltpu.SemaphoreType.DMA
    spec = pl.BlockSpec(memory_space=pltpu.VMEM)
    return pl.pallas_call(
        functools.partial(kernel, n_dp, n_space, count),
        out_shape=(
            jax.ShapeDtypeStruct(cotangent.shape, BF16),
            jax.ShapeDtypeStruct(image.shape, BF16),
            jax.ShapeDtypeStruct(weight.shape, F32),
            jax.ShapeDtypeStruct(weight.shape, F32),
            jax.ShapeDtypeStruct(weight.shape, F32),
        ),
        in_specs=[spec] * 5,
        out_specs=[spec] * 5,
        scratch_shapes=[
            vmem((2, rows * cols + 24, 128), F32),
            vmem((2, rows * cols + 24, 128), F32),
            vmem((2, positions + 8, 128), F32),
            vmem((2, positions + 8, 128), F32),
            vmem((2 * cols, C), BF16),
            vmem((2 * cols, C), BF16),
            vmem((cols, C), BF16),
            vmem((cols, C), BF16),
            vmem((n_dp, 2, half, wide), BF16),
            vmem((9, positions, C), BF16),
            vmem((n_dp, half, wide), F32),
            vmem((n_dp, half, wide), BF16),
            vmem((n_dp, half, wide), BF16),
            vmem((n_dp, half, wide), F32),
            vmem((n_dp, half, wide), BF16),
            vmem((n_dp, half, wide), BF16),
            vmem((nz, half, 128), F32),
            vmem((nz, half, 128), BF16),
            vmem((nz, half, 128), BF16),
            vmem((n_space, half, 128), BF16),
            vmem((C, wide), F32),
            dma((2,)), dma((2,)),
            dma((n_dp,)), dma((n_dp,)), dma((n_dp,)), dma((n_dp,)),
            dma((1,)), dma((1,)),
            dma((n_dp,)), dma((n_dp,)),
            dma((nz,)), dma((nz,)),
            dma((n_space,)), dma((n_space,)),
        ],
        compiler_params=pltpu.CompilerParams(
            collective_id=0, has_side_effects=True, vmem_limit_bytes=48 * 1024 * 1024
        ),
    )(image, cotangent, weight, moment_one, moment_two)


def solution(mesh):
    whole = P("dp", "space", None)
    rows = P("dp", None)
    specs = (whole, whole, rows, rows, rows)
    return jax.shard_map(
        functools.partial(body, mesh.shape["dp"], mesh.shape["space"]),
        mesh=mesh, in_specs=specs, out_specs=specs, check_vma=False)
```

```python
import functools

import jax
import jax.numpy as jnp
from jax import lax
from jax.experimental import pallas as pl
from jax.experimental.pallas import tpu as pltpu
from jax.sharding import PartitionSpec as P

MESH = pl.DeviceIdType.MESH
F32 = jnp.float32
BF16 = jnp.bfloat16

beta_one = 0.9
beta_two = 0.999
learn_rate = 0.01
decay_rate = 0.01
epsilon = 1e-08
adam_step = 10


def up(value, unit):
    return -(-value // unit) * unit


def kernel(
    n_dp, n_space,
    image_hbm, cotangent_hbm, weight_hbm, one_hbm, two_hbm,
    out, grad_image, gradient, weight, one, two,
    image, cotangent, kern, even, odd, cot, cot_next, img_edge_out, img_edge_in, cot_edge_out, cot_edge_in,
    wt, taps, part, mate_out, mate_in, own, dp_out, dp_in, shares, z_out, z_in, final,
    load,    edge_send, edge_recv, w_send, w_recv, wm_send, wm_recv, m_send, m_recv,
    d_send, d_recv, z_send, z_recv, f_send, f_recv,
):
    C, shard = weight.shape
    half = C // 2
    rest = C - 128
    wide = wt.shape[-1]
    cols = out.shape[2] // C
    out_rows = out.shape[1]
    rows = image.shape[1]
    positions = cols * out_rows
    nz = n_space // 2
    blocks = wide // 128
    dp = lax.axis_index("dp")
    space = lax.axis_index("space")
    core = lax.rem(space, 2)
    zi = lax.div(space, 2)
    mate = space + 1 - 2 * core

    loads = [pltpu.make_async_copy(src, dst, load.at[n]) for n, (src, dst) in enumerate(
        ((cotangent_hbm, cotangent), (image_hbm, image), (weight_hbm, weight), (one_hbm, one), (two_hbm, two)))]
    for copy in loads:
        copy.start()

    barrier = pltpu.get_barrier_semaphore()
    for k in range(1, n_dp):
        pl.semaphore_signal(barrier, inc=1, device_id=(lax.rem(dp + k, n_dp), space), device_id_type=MESH)
    for k in range(1, n_space):
        pl.semaphore_signal(barrier, inc=1, device_id=(dp, lax.rem(space + k, n_space)), device_id_type=MESH)

    def remote(src, dst, send, recv, to_dp, to_space):
        return pltpu.make_async_remote_copy(
            src_ref=src, dst_ref=dst, send_sem=send, recv_sem=recv,
            device_id=(to_dp, to_space), device_id_type=MESH)

    zeros_e = jnp.zeros(even.shape[1:], F32)
    even[1] = zeros_e
    odd[1] = zeros_e
    odd[0, 0:16, :] = jnp.zeros((16, 128), F32)
    cot[1] = jnp.zeros(cot.shape[1:], F32)
    cot[0, pl.ds(positions, 8), :] = jnp.zeros((8, 128), F32)
    cot_next[0, pl.ds(positions, 8), :] = jnp.zeros((8, 128), F32)
    cot_next[1, pl.ds(positions, 8), :] = jnp.zeros((8, 128), F32)

    group = 4 * C

    def split_cot(g, carry):
        v = cotangent[0, :, pl.ds(pl.multiple_of(g * group, 128), group)].astype(F32)
        pieces = [v[:, k * C : (k + 1) * C] for k in range(4)]
        for k in range(0, 4, 2):
            both = jnp.concatenate([pieces[k], pieces[k + 1]], axis=0)
            at = pl.multiple_of((4 * g + k) * out_rows, 8)
            cot[0, pl.ds(at, 8), :] = both[:, :128]
            cot[1, pl.ds(at, 8), 0:rest] = both[:, 128:]
        return carry

    loads[0].wait()
    lax.fori_loop(0, cols // 4, split_cot, 0)

    def split_image(g, carry):
        v = image[0, :, pl.ds(pl.multiple_of(g * group, 128), group)].astype(F32)
        for k in range(4):
            piece = v[:, k * C : (k + 1) * C]
            ref = odd if k % 2 else even
            at = pl.multiple_of((2 * g + k // 2) * rows + 16, 8)
            ref[0, pl.ds(at, rows), :] = piece[:, :128]
            ref[1, pl.ds(at, rows), 0:rest] = piece[:, 128:]
        return carry

    loads[1].wait()
    lax.fori_loop(0, cols // 2, split_image, 0)

    def strided(ref, start, size, stride):
        at = pl.ds(start, size, stride=stride)
        return jnp.concatenate([ref[0, at, :], ref[1, at, :]], axis=1)[:, :C]

    img_edge_out[0:cols] = strided(even, 16 + rows - 1, cols, rows).astype(BF16)
    img_edge_out[cols : 2 * cols] = strided(odd, 16 + rows - 1, cols, rows).astype(BF16)
    cot_edge_out[...] = strided(cot, 0, cols, out_rows).astype(BF16)

    loads[2].wait()
    mine = weight[...].astype(BF16)
    wt[dp, 0, :, 0:shard] = mine[:half]
    wt[dp, 1, :, 0:shard] = mine[half:]

    pl.semaphore_wait(barrier, n_dp + n_space - 2)

    img_copy = remote(img_edge_out, img_edge_in, edge_send.at[0], edge_recv.at[0], dp, lax.rem(space + 1, n_space))
    cot_copy = remote(cot_edge_out, cot_edge_in, edge_send.at[1], edge_recv.at[1], dp, lax.rem(space + n_space - 1, n_space))

    @pl.when(space < n_space - 1)
    def _():
        img_copy.start()

    @pl.when(space > 0)
    def _():
        cot_copy.start()

    def w_copy(k):
        return remote(wt.at[dp, core], wt.at[dp, core], w_send.at[k], w_recv.at[k], lax.rem(dp + k, n_dp), space)

    for k in range(1, n_dp):
        w_copy(k).start()

    whole_cot = strided(cot, 0, positions, 1)
    cot_t = whole_cot.T.astype(BF16)
    first, second = cot_t[:half], cot_t[half:]
    lower = core == 0
    mate_rows = jnp.where(lower, second.astype(F32), first.astype(F32)).astype(BF16)
    own_rows = jnp.where(lower, first.astype(F32), second.astype(F32)).astype(BF16)

    def patch(r, s):
        ref = even if s == 1 else odd
        start = 16 + r - 1 - (rows if s == 0 else 0)
        return strided(ref, start, positions, 2).astype(BF16)

    def place(ref, tap, value, by_shard):
        lo = tap * C
        end = lo + C
        while lo < end:
            d = lo // shard
            stop = min(end, (d + 1) * shard)
            ref[d, :, lo - d * shard : stop - d * shard] = value[:, lo - tap * C : stop - tap * C]
            lo = stop

    for d in range(n_dp):
        if wide > shard:
            pad = jnp.zeros((half, wide - shard), F32)
            own[d, :, shard:wide] = pad
            part[d, :, shard:wide] = pad

    def grads(r):
        for s in range(3):
            p = patch(r, s)
            taps[3 * r + s] = p
            place(part, 3 * r + s, jnp.dot(mate_rows, p, preferred_element_type=F32), True)

    grads(1)
    grads(2)
    cut = -(-3 * C // shard)

    def mate_copy(n):
        at = pl.ds(0, cut) if n else pl.ds(cut, n_dp - cut)
        return remote(mate_out.at[at], mate_in.at[at], m_send.at[n], m_recv.at[n], dp, mate)

    mate_out[cut:] = part[cut:].astype(BF16)
    mate_copy(0).start()

    @pl.when(space < n_space - 1)
    def _():
        img_copy.wait_send()

    @pl.when(space > 0)
    def _():
        img_copy.wait_recv()

    @pl.when(space == 0)
    def _():
        img_edge_in[...] = jnp.zeros(img_edge_in.shape, BF16)

    for base, ref in ((0, even), (cols, odd)):
        edge = img_edge_in[base : base + cols].astype(F32)
        at = pl.ds(15, cols, stride=rows)
        ref[0, at, :] = edge[:, :128]
        ref[1, at, :] = jnp.concatenate([edge[:, 128:], jnp.zeros((cols, 256 - C), F32)], axis=1)
    grads(0)
    mate_out[:cut] = part[:cut].astype(BF16)
    mate_copy(1).start()

    def wm_copy(k):
        src = lax.rem(dp + n_dp - k, n_dp)
        return remote(wt.at[src, core], wt.at[src, core], wm_send.at[k], wm_recv.at[k], dp, mate)

    for t in (3, 4, 5, 6, 7, 8, 0, 1, 2):
        place(own, t, jnp.dot(own_rows, taps[t], preferred_element_type=F32), True)

    mate_copy(0).wait()
    mate_copy(1).wait()
    own[...] = own[...] + mate_in[...].astype(F32)

    dp_out[...] = own[...].astype(BF16)

    def d_copy(k):
        to = lax.rem(dp + k, n_dp)
        return remote(dp_out.at[to], dp_in.at[k], d_send.at[k], d_recv.at[k], to, space)

    for k in range(1, n_dp):
        d_copy(k).start()

    for k in range(1, n_dp):
        w_copy(k).wait()
        wm_copy(k).start()

    def keep(ref, at, value):
        ref[0, at, :] = value[:, :128]
        ref[1, at, :] = jnp.concatenate([value[:, 128:], jnp.zeros((value.shape[0], 256 - C), F32)], axis=1)

    @pl.when(space > 0)
    def _():
        cot_copy.wait_send()

    @pl.when(space < n_space - 1)
    def _():
        cot_copy.wait_recv()

    @pl.when(space == n_space - 1)
    def _():
        cot_edge_in[...] = jnp.zeros(cot_edge_in.shape, BF16)

    for h in range(2):
        cot_next[h, pl.ds(0, positions), :] = cot[h, pl.ds(1, positions), :]
    edge = cot_edge_in[...].astype(F32)
    at = pl.ds(out_rows - 1, cols, stride=out_rows)
    keep(cot_next, at, edge)
    for k in range(1, n_dp):
        wm_copy(k).wait()

    def tap_t(t):
        lo = t * C
        end = lo + C
        pieces = []
        while lo < end:
            d = lo // shard
            stop = min(end, (d + 1) * shard)
            at = slice(lo - d * shard, stop - d * shard)
            pieces.append(jnp.concatenate([wt[d, 0, :, at], wt[d, 1, :, at]], axis=0).astype(F32))
            lo = stop
        value = pieces[0] if len(pieces) == 1 else jnp.concatenate(pieces, axis=1)
        return value.astype(BF16)

    for t in range(9):
        kern[t] = tap_t(t)
    acc = jnp.zeros((positions, C), F32)
    for t in range(9):
        acc = acc + lax.dot_general(taps[t], kern[t], (((1,), (1,)), ((), ())), preferred_element_type=F32)

    keep(even, pl.ds(0, positions), acc)

    def join_out(g, carry):
        pieces = []
        for k in range(0, 4, 2):
            at = pl.multiple_of((4 * g + k) * out_rows, 8)
            v = jnp.concatenate([even[0, pl.ds(at, 8), :], even[1, pl.ds(at, 8), 0:rest]], axis=1)
            pieces += [v[:out_rows], v[out_rows:]]
        out[0, :, pl.ds(pl.multiple_of(g * group, 128), group)] = jnp.concatenate(pieces, axis=1).astype(BF16)
        return carry

    lax.fori_loop(0, cols // 4, join_out, 0)

    summed = own[dp]
    for k in range(1, n_dp):
        d_copy(k).wait()
        summed = summed + dp_in[k].astype(F32)
    pieces = [summed[:, b * 128 : (b + 1) * 128] for b in range(blocks)]
    height = blocks * half
    if nz * shares.shape[1] > height:
        pieces.append(jnp.zeros((nz * shares.shape[1] - height, 128), F32))
    stacked = jnp.concatenate(pieces, axis=0).reshape(shares.shape)
    shares[...] = stacked
    z_out[...] = stacked.astype(BF16)

    def z_copy(k):
        to = lax.rem(zi + k, nz)
        return remote(z_out.at[to], z_in.at[k], z_send.at[k], z_recv.at[k], dp, 2 * to + core)

    for k in range(1, nz):
        z_copy(k).start()
    here = whole_cot.astype(BF16)
    right = strided(cot, out_rows, positions, 1).astype(BF16)
    below = strided(cot_next, 0, positions, 1).astype(BF16)
    both = strided(cot_next, out_rows, positions, 1).astype(BF16)

    def back(c, r, s):
        return jnp.dot(c, kern[3 * r + s], preferred_element_type=F32)

    keep(even, pl.ds(0, positions, stride=2), back(here, 1, 1))
    keep(even, pl.ds(1, positions, stride=2), back(here, 2, 1) + back(below, 0, 1))
    summed = shares[zi]
    for k in range(1, nz):
        z_copy(k).wait()
        summed = summed + z_in[k].astype(F32)

    final[space] = summed.astype(BF16)

    def f_copy(k):
        return remote(final.at[space], final.at[space], f_send.at[k], f_recv.at[k], dp, lax.rem(space + k, n_space))

    for k in range(1, n_space):
        f_copy(k).start()
    keep(odd, pl.ds(0, positions, stride=2), back(here, 1, 2) + back(right, 1, 0))
    keep(odd, pl.ds(1, positions, stride=2),
         back(here, 2, 2) + back(right, 2, 0) + back(below, 0, 2) + back(both, 0, 0))

    def join_grad(g, carry):
        pieces = []
        for k in range(4):
            ref = odd if k % 2 else even
            at = pl.multiple_of((2 * g + k // 2) * rows, 8)
            pieces.append(jnp.concatenate([ref[0, pl.ds(at, rows), :], ref[1, pl.ds(at, rows), 0:rest]], axis=1))
        grad_image[0, :, pl.ds(pl.multiple_of(g * group, 128), group)] = jnp.concatenate(pieces, axis=1).astype(BF16)
        return carry

    lax.fori_loop(0, cols // 2, join_grad, 0)

    for k in range(1, n_space):
        f_copy(k).wait()
    gradient[...] = final[...]
    loads[3].wait()
    loads[4].wait()


def finish(count, out_in, grad_in, gradient, weight, moment_one, moment_two,
           out, grad_image, new_weight, new_one, new_two, w_buf, one_buf, two_buf, sems):
    C, shard = weight.shape
    half = C // 2
    copies = [pltpu.make_async_copy(out_in, out, sems.at[0]),
              pltpu.make_async_copy(grad_in, grad_image, sems.at[1])]
    for copy in copies:
        copy.start()
    blocks = up(shard, 128) // 128
    halves = []
    for c in range(2):
        stacked = jnp.concatenate([gradient[n].astype(F32) for n in range(c, gradient.shape[0], 2)], axis=0)
        halves.append(jnp.concatenate([stacked[b * half : (b + 1) * half] for b in range(blocks)], axis=1))
    grad = jnp.concatenate(halves, axis=0)[:, :shard] / float(count)
    one = beta_one * moment_one[...] + (1.0 - beta_one) * grad
    one_buf[...] = one
    copies.append(pltpu.make_async_copy(one_buf, new_one, sems.at[2]))
    copies[-1].start()
    two = beta_two * moment_two[...] + (1.0 - beta_two) * grad * grad
    two_buf[...] = two
    copies.append(pltpu.make_async_copy(two_buf, new_two, sems.at[3]))
    copies[-1].start()
    first_hat = one / (1.0 - beta_one**adam_step)
    second_hat = two / (1.0 - beta_two**adam_step)
    old = weight[...]
    w_buf[...] = old - learn_rate * (first_hat / (jnp.sqrt(second_hat) + epsilon) + decay_rate * old)
    copies.append(pltpu.make_async_copy(w_buf, new_weight, sems.at[4]))
    copies[-1].start()
    for copy in copies:
        copy.wait()


def body(n_dp, n_space, image, cotangent, weight, moment_one, moment_two):
    shard, C = weight.shape
    half = C // 2
    wide = up(shard, 128)
    rows = image.shape[1]
    out_rows = cotangent.shape[1]
    cols = cotangent.shape[2] // C
    positions = out_rows * cols
    nz = n_space // 2
    count = positions * n_dp * n_space
    vmem = pltpu.VMEM
    dma = pltpu.SemaphoreType.DMA
    spec = pl.BlockSpec(memory_space=pltpu.VMEM)
    hbm = pl.BlockSpec(memory_space=pltpu.HBM)
    share = up(up(wide * half // 128, nz) // nz, 16)
    weight_t = weight.T
    state = jax.ShapeDtypeStruct(weight_t.shape, F32)
    out, grad_image, gradient, *held = pl.pallas_call(
        functools.partial(kernel, n_dp, n_space),
        out_shape=(
            jax.ShapeDtypeStruct(cotangent.shape, BF16),
            jax.ShapeDtypeStruct(image.shape, BF16),
            jax.ShapeDtypeStruct((n_space, share, 128), BF16),
            state, state, state,
        ),
        in_specs=[hbm] * 5,
        out_specs=[spec] * 6,
        scratch_shapes=[
            vmem(image.shape, BF16),
            vmem(cotangent.shape, BF16),
            vmem((9, C, C), BF16),
            vmem((2, rows * cols + 24, 128), F32),
            vmem((2, rows * cols + 24, 128), F32),
            vmem((2, positions + 8, 128), F32),
            vmem((2, positions + 8, 128), F32),
            vmem((2 * cols, C), BF16),
            vmem((2 * cols, C), BF16),
            vmem((cols, C), BF16),
            vmem((cols, C), BF16),
            vmem((n_dp, 2, half, wide), BF16),
            vmem((9, positions, C), BF16),
            vmem((n_dp, half, wide), F32),
            vmem((n_dp, half, wide), BF16),
            vmem((n_dp, half, wide), BF16),
            vmem((n_dp, half, wide), F32),
            vmem((n_dp, half, wide), BF16),
            vmem((n_dp, half, wide), BF16),
            vmem((nz, share, 128), F32),
            vmem((nz, share, 128), BF16),
            vmem((nz, share, 128), BF16),
            vmem((n_space, share, 128), BF16),
            dma((5,)),
            dma((2,)), dma((2,)),
            dma((n_dp,)), dma((n_dp,)), dma((n_dp,)), dma((n_dp,)),
            dma((2,)), dma((2,)),
            dma((n_dp,)), dma((n_dp,)),
            dma((nz,)), dma((nz,)),
            dma((n_space,)), dma((n_space,)),
        ],
        compiler_params=pltpu.CompilerParams(
            collective_id=0, has_side_effects=True, vmem_limit_bytes=24 * 1024 * 1024
        ),
    )(image, cotangent, weight_t, moment_one.T, moment_two.T)
    out, grad_image, new_weight, new_one, new_two = pl.pallas_call(
        functools.partial(finish, count),
        out_shape=(
            jax.ShapeDtypeStruct(cotangent.shape, BF16),
            jax.ShapeDtypeStruct(image.shape, BF16),
            state, state, state,
        ),
        in_specs=[spec] * 6,
        out_specs=[hbm] * 5,
        scratch_shapes=[vmem(weight_t.shape, F32)] * 3 + [dma((5,))],
        compiler_params=pltpu.CompilerParams(vmem_limit_bytes=16 * 1024 * 1024),
    )(out, grad_image, gradient, *held)
    return out, grad_image, new_weight.T, new_one.T, new_two.T


def solution(mesh):
    whole = P("dp", "space", None)
    rows = P("dp", None)
    specs = (whole, whole, rows, rows, rows)
    return jax.shard_map(
        functools.partial(body, mesh.shape["dp"], mesh.shape["space"]),
        mesh=mesh, in_specs=specs, out_specs=specs, check_vma=False)
```

```python
import functools

import jax
import jax.numpy as jnp
from jax import lax
from jax.experimental import pallas as pl
from jax.experimental.pallas import tpu as pltpu
from jax.sharding import PartitionSpec as P

MESH = pl.DeviceIdType.MESH
F32 = jnp.float32
BF16 = jnp.bfloat16

beta_one = 0.9
beta_two = 0.999
learn_rate = 0.01
decay_rate = 0.01
epsilon = 1e-08
adam_step = 10


def up(value, unit):
    return -(-value // unit) * unit


def kernel(
    n_dp, n_space,
    image_hbm, cotangent_hbm, weight_hbm, one_hbm, two_hbm,
    out, grad_image, gradient, weight, one, two,
    image, cotangent, kern, even, odd, cot, cot_next, img_edge_out, img_edge_in, cot_edge_out, cot_edge_in,
    wt, taps, part, mate_out, mate_in, own, dp_out, dp_in, shares, z_out, z_in, final,
    load,    edge_send, edge_recv, w_send, w_recv, wm_send, wm_recv, m_send, m_recv,
    d_send, d_recv, z_send, z_recv, f_send, f_recv,
):
    C, shard = weight.shape
    half = C // 2
    rest = C - 128
    wide = wt.shape[-1]
    cols = out.shape[2] // C
    out_rows = out.shape[1]
    rows = image.shape[1]
    positions = cols * out_rows
    nz = n_space // 2
    blocks = wide // 128
    dp = lax.axis_index("dp")
    space = lax.axis_index("space")
    core = lax.rem(space, 2)
    zi = lax.div(space, 2)
    mate = space + 1 - 2 * core

    loads = [pltpu.make_async_copy(src, dst, load.at[n]) for n, (src, dst) in enumerate(
        ((cotangent_hbm, cotangent), (image_hbm, image), (weight_hbm, weight), (one_hbm, one), (two_hbm, two)))]
    for copy in loads:
        copy.start()

    barrier = pltpu.get_barrier_semaphore()
    for k in range(1, n_dp):
        pl.semaphore_signal(barrier, inc=1, device_id=(lax.rem(dp + k, n_dp), space), device_id_type=MESH)
    for k in range(1, n_space):
        pl.semaphore_signal(barrier, inc=1, device_id=(dp, lax.rem(space + k, n_space)), device_id_type=MESH)

    def remote(src, dst, send, recv, to_dp, to_space):
        return pltpu.make_async_remote_copy(
            src_ref=src, dst_ref=dst, send_sem=send, recv_sem=recv,
            device_id=(to_dp, to_space), device_id_type=MESH)

    zeros_e = jnp.zeros(even.shape[1:], F32)
    even[1] = zeros_e
    odd[1] = zeros_e
    odd[0, 0:16, :] = jnp.zeros((16, 128), F32)
    cot[1] = jnp.zeros(cot.shape[1:], F32)
    cot[0, pl.ds(positions, 8), :] = jnp.zeros((8, 128), F32)
    cot_next[0, pl.ds(positions, 8), :] = jnp.zeros((8, 128), F32)
    cot_next[1, pl.ds(positions, 8), :] = jnp.zeros((8, 128), F32)

    group = 4 * C

    def split_cot(g, carry):
        v = cotangent[0, :, pl.ds(pl.multiple_of(g * group, 128), group)].astype(F32)
        pieces = [v[:, k * C : (k + 1) * C] for k in range(4)]
        for k in range(0, 4, 2):
            both = jnp.concatenate([pieces[k], pieces[k + 1]], axis=0)
            at = pl.multiple_of((4 * g + k) * out_rows, 8)
            cot[0, pl.ds(at, 8), :] = both[:, :128]
            cot[1, pl.ds(at, 8), 0:rest] = both[:, 128:]
        return carry

    loads[0].wait()
    lax.fori_loop(0, cols // 4, split_cot, 0)

    def split_image(g, carry):
        v = image[0, :, pl.ds(pl.multiple_of(g * group, 128), group)].astype(F32)
        for k in range(4):
            piece = v[:, k * C : (k + 1) * C]
            ref = odd if k % 2 else even
            at = pl.multiple_of((2 * g + k // 2) * rows + 16, 8)
            ref[0, pl.ds(at, rows), :] = piece[:, :128]
            ref[1, pl.ds(at, rows), 0:rest] = piece[:, 128:]
        return carry

    loads[1].wait()
    lax.fori_loop(0, cols // 2, split_image, 0)

    def strided(ref, start, size, stride):
        at = pl.ds(start, size, stride=stride)
        return jnp.concatenate([ref[0, at, :], ref[1, at, :]], axis=1)[:, :C]

    img_edge_out[0:cols] = strided(even, 16 + rows - 1, cols, rows).astype(BF16)
    img_edge_out[cols : 2 * cols] = strided(odd, 16 + rows - 1, cols, rows).astype(BF16)
    cot_edge_out[...] = strided(cot, 0, cols, out_rows).astype(BF16)

    loads[2].wait()
    mine = weight[...].astype(BF16)
    wt[dp, 0, :, 0:shard] = mine[:half]
    wt[dp, 1, :, 0:shard] = mine[half:]

    pl.semaphore_wait(barrier, n_dp + n_space - 2)

    img_copy = remote(img_edge_out, img_edge_in, edge_send.at[0], edge_recv.at[0], dp, lax.rem(space + 1, n_space))
    cot_copy = remote(cot_edge_out, cot_edge_in, edge_send.at[1], edge_recv.at[1], dp, lax.rem(space + n_space - 1, n_space))

    @pl.when(space < n_space - 1)
    def _():
        img_copy.start()

    @pl.when(space > 0)
    def _():
        cot_copy.start()

    def w_copy(k):
        return remote(wt.at[dp, core], wt.at[dp, core], w_send.at[k], w_recv.at[k], lax.rem(dp + k, n_dp), space)

    for k in range(1, n_dp):
        w_copy(k).start()

    whole_cot = strided(cot, 0, positions, 1)
    cot_t = whole_cot.T.astype(BF16)
    first, second = cot_t[:half], cot_t[half:]
    lower = core == 0
    mate_rows = jnp.where(lower, second.astype(F32), first.astype(F32)).astype(BF16)
    own_rows = jnp.where(lower, first.astype(F32), second.astype(F32)).astype(BF16)

    def patch(r, s):
        ref = even if s == 1 else odd
        start = 16 + r - 1 - (rows if s == 0 else 0)
        return strided(ref, start, positions, 2).astype(BF16)

    def place(ref, tap, value, by_shard):
        lo = tap * C
        end = lo + C
        while lo < end:
            d = lo // shard
            stop = min(end, (d + 1) * shard)
            ref[d, :, lo - d * shard : stop - d * shard] = value[:, lo - tap * C : stop - tap * C]
            lo = stop

    for d in range(n_dp):
        if wide > shard:
            pad = jnp.zeros((half, wide - shard), F32)
            own[d, :, shard:wide] = pad
            part[d, :, shard:wide] = pad

    def grads(r):
        for s in range(3):
            p = patch(r, s)
            taps[3 * r + s] = p
            place(part, 3 * r + s, jnp.dot(mate_rows, p, preferred_element_type=F32), True)

    grads(1)
    grads(2)
    cut = -(-3 * C // shard)

    def mate_copy(n):
        at = pl.ds(0, cut) if n else pl.ds(cut, n_dp - cut)
        return remote(mate_out.at[at], mate_in.at[at], m_send.at[n], m_recv.at[n], dp, mate)

    mate_out[cut:] = part[cut:].astype(BF16)
    mate_copy(0).start()

    @pl.when(space < n_space - 1)
    def _():
        img_copy.wait_send()

    @pl.when(space > 0)
    def _():
        img_copy.wait_recv()

    @pl.when(space == 0)
    def _():
        img_edge_in[...] = jnp.zeros(img_edge_in.shape, BF16)

    for base, ref in ((0, even), (cols, odd)):
        edge = img_edge_in[base : base + cols].astype(F32)
        at = pl.ds(15, cols, stride=rows)
        ref[0, at, :] = edge[:, :128]
        ref[1, at, :] = jnp.concatenate([edge[:, 128:], jnp.zeros((cols, 256 - C), F32)], axis=1)
    grads(0)
    mate_out[:cut] = part[:cut].astype(BF16)
    mate_copy(1).start()

    def wm_copy(k):
        src = lax.rem(dp + n_dp - k, n_dp)
        return remote(wt.at[src, core], wt.at[src, core], wm_send.at[k], wm_recv.at[k], dp, mate)

    for t in (3, 4, 5, 6, 7, 8, 0, 1, 2):
        place(own, t, jnp.dot(own_rows, taps[t], preferred_element_type=F32), True)

    mate_copy(0).wait()
    mate_copy(1).wait()
    own[...] = own[...] + mate_in[...].astype(F32)

    dp_out[...] = own[...].astype(BF16)

    def d_copy(k):
        to = lax.rem(dp + k, n_dp)
        return remote(dp_out.at[to], dp_in.at[k], d_send.at[k], d_recv.at[k], to, space)

    for k in range(1, n_dp):
        d_copy(k).start()

    for k in range(1, n_dp):
        w_copy(k).wait()
        wm_copy(k).start()

    def keep(ref, at, value):
        ref[0, at, :] = value[:, :128]
        ref[1, at, :] = jnp.concatenate([value[:, 128:], jnp.zeros((value.shape[0], 256 - C), F32)], axis=1)

    @pl.when(space > 0)
    def _():
        cot_copy.wait_send()

    @pl.when(space < n_space - 1)
    def _():
        cot_copy.wait_recv()

    @pl.when(space == n_space - 1)
    def _():
        cot_edge_in[...] = jnp.zeros(cot_edge_in.shape, BF16)

    for h in range(2):
        cot_next[h, pl.ds(0, positions), :] = cot[h, pl.ds(1, positions), :]
    edge = cot_edge_in[...].astype(F32)
    at = pl.ds(out_rows - 1, cols, stride=out_rows)
    keep(cot_next, at, edge)
    for k in range(1, n_dp):
        wm_copy(k).wait()

    def tap_t(t):
        lo = t * C
        end = lo + C
        pieces = []
        while lo < end:
            d = lo // shard
            stop = min(end, (d + 1) * shard)
            at = slice(lo - d * shard, stop - d * shard)
            pieces.append(jnp.concatenate([wt[d, 0, :, at], wt[d, 1, :, at]], axis=0).astype(F32))
            lo = stop
        value = pieces[0] if len(pieces) == 1 else jnp.concatenate(pieces, axis=1)
        return value.astype(BF16)

    for t in range(9):
        kern[t] = tap_t(t)
    acc = jnp.zeros((positions, C), F32)
    for t in range(9):
        acc = acc + lax.dot_general(taps[t], kern[t], (((1,), (1,)), ((), ())), preferred_element_type=F32)

    keep(even, pl.ds(0, positions), acc)

    def join_out(g, carry):
        pieces = []
        for k in range(0, 4, 2):
            at = pl.multiple_of((4 * g + k) * out_rows, 8)
            v = jnp.concatenate([even[0, pl.ds(at, 8), :], even[1, pl.ds(at, 8), 0:rest]], axis=1)
            pieces += [v[:out_rows], v[out_rows:]]
        out[0, :, pl.ds(pl.multiple_of(g * group, 128), group)] = jnp.concatenate(pieces, axis=1).astype(BF16)
        return carry

    lax.fori_loop(0, cols // 4, join_out, 0)

    summed = own[dp]
    for k in range(1, n_dp):
        d_copy(k).wait()
        summed = summed + dp_in[k].astype(F32)
    pieces = [summed[:, b * 128 : (b + 1) * 128] for b in range(blocks)]
    height = blocks * half
    if nz * shares.shape[1] > height:
        pieces.append(jnp.zeros((nz * shares.shape[1] - height, 128), F32))
    stacked = jnp.concatenate(pieces, axis=0).reshape(shares.shape)
    shares[...] = stacked
    z_out[...] = stacked.astype(BF16)

    def z_copy(k):
        to = lax.rem(zi + k, nz)
        return remote(z_out.at[to], z_in.at[k], z_send.at[k], z_recv.at[k], dp, 2 * to + core)

    for k in range(1, nz):
        z_copy(k).start()
    here = whole_cot.astype(BF16)
    right = strided(cot, out_rows, positions, 1).astype(BF16)
    below = strided(cot_next, 0, positions, 1).astype(BF16)
    both = strided(cot_next, out_rows, positions, 1).astype(BF16)

    def back(c, r, s):
        return jnp.dot(c, kern[3 * r + s], preferred_element_type=F32)

    keep(even, pl.ds(0, positions, stride=2), back(here, 1, 1))
    keep(even, pl.ds(1, positions, stride=2), back(here, 2, 1) + back(below, 0, 1))
    summed = shares[zi]
    for k in range(1, nz):
        z_copy(k).wait()
        summed = summed + z_in[k].astype(F32)

    final[space] = summed.astype(BF16)

    def f_copy(k):
        return remote(final.at[space], final.at[space], f_send.at[k], f_recv.at[k], dp, lax.rem(space + k, n_space))

    for k in range(1, n_space):
        f_copy(k).start()
    keep(odd, pl.ds(0, positions, stride=2), back(here, 1, 2) + back(right, 1, 0))
    keep(odd, pl.ds(1, positions, stride=2),
         back(here, 2, 2) + back(right, 2, 0) + back(below, 0, 2) + back(both, 0, 0))

    def join_grad(g, carry):
        pieces = []
        for k in range(4):
            ref = odd if k % 2 else even
            at = pl.multiple_of((2 * g + k // 2) * rows, 8)
            pieces.append(jnp.concatenate([ref[0, pl.ds(at, rows), :], ref[1, pl.ds(at, rows), 0:rest]], axis=1))
        grad_image[0, :, pl.ds(pl.multiple_of(g * group, 128), group)] = jnp.concatenate(pieces, axis=1).astype(BF16)
        return carry

    lax.fori_loop(0, cols // 2, join_grad, 0)

    for k in range(1, n_space):
        f_copy(k).wait()
    gradient[...] = final[...]
    loads[3].wait()
    loads[4].wait()


def finish(count, out_in, grad_in, gradient, weight, moment_one, moment_two,
           out, grad_image, new_weight, new_one, new_two, w_buf, one_buf, two_buf, sems):
    C, shard = weight.shape
    half = C // 2
    copies = [pltpu.make_async_copy(out_in, out, sems.at[0]),
              pltpu.make_async_copy(grad_in, grad_image, sems.at[1])]
    for copy in copies:
        copy.start()
    blocks = up(shard, 128) // 128
    halves = []
    for c in range(2):
        stacked = jnp.concatenate([gradient[n].astype(F32) for n in range(c, gradient.shape[0], 2)], axis=0)
        halves.append(jnp.concatenate([stacked[b * half : (b + 1) * half] for b in range(blocks)], axis=1))
    grad = jnp.concatenate(halves, axis=0)[:, :shard] / float(count)
    one = beta_one * moment_one[...] + (1.0 - beta_one) * grad
    one_buf[...] = one
    copies.append(pltpu.make_async_copy(one_buf, new_one, sems.at[2]))
    copies[-1].start()
    two = beta_two * moment_two[...] + (1.0 - beta_two) * grad * grad
    two_buf[...] = two
    copies.append(pltpu.make_async_copy(two_buf, new_two, sems.at[3]))
    copies[-1].start()
    first_hat = one / (1.0 - beta_one**adam_step)
    second_hat = two / (1.0 - beta_two**adam_step)
    old = weight[...]
    w_buf[...] = old - learn_rate * (first_hat / (jnp.sqrt(second_hat) + epsilon) + decay_rate * old)
    copies.append(pltpu.make_async_copy(w_buf, new_weight, sems.at[4]))
    copies[-1].start()
    for copy in copies:
        copy.wait()


def body(n_dp, n_space, image, cotangent, weight, moment_one, moment_two):
    shard, C = weight.shape
    half = C // 2
    wide = up(shard, 128)
    rows = image.shape[1]
    out_rows = cotangent.shape[1]
    cols = cotangent.shape[2] // C
    positions = out_rows * cols
    nz = n_space // 2
    count = positions * n_dp * n_space
    vmem = pltpu.VMEM
    dma = pltpu.SemaphoreType.DMA
    spec = pl.BlockSpec(memory_space=pltpu.VMEM)
    hbm = pl.BlockSpec(memory_space=pltpu.HBM)
    share = up(up(wide * half // 128, nz) // nz, 16)
    weight_t = weight.T
    state = jax.ShapeDtypeStruct(weight_t.shape, F32)
    out, grad_image, gradient, *held = pl.pallas_call(
        functools.partial(kernel, n_dp, n_space),
        out_shape=(
            jax.ShapeDtypeStruct(cotangent.shape, BF16),
            jax.ShapeDtypeStruct(image.shape, BF16),
            jax.ShapeDtypeStruct((n_space, share, 128), BF16),
            state, state, state,
        ),
        in_specs=[hbm] * 5,
        out_specs=[spec] * 6,
        scratch_shapes=[
            vmem(image.shape, BF16),
            vmem(cotangent.shape, BF16),
            vmem((9, C, C), BF16),
            vmem((2, rows * cols + 24, 128), F32),
            vmem((2, rows * cols + 24, 128), F32),
            vmem((2, positions + 8, 128), F32),
            vmem((2, positions + 8, 128), F32),
            vmem((2 * cols, C), BF16),
            vmem((2 * cols, C), BF16),
            vmem((cols, C), BF16),
            vmem((cols, C), BF16),
            vmem((n_dp, 2, half, wide), BF16),
            vmem((9, positions, C), BF16),
            vmem((n_dp, half, wide), F32),
            vmem((n_dp, half, wide), BF16),
            vmem((n_dp, half, wide), BF16),
            vmem((n_dp, half, wide), F32),
            vmem((n_dp, half, wide), BF16),
            vmem((n_dp, half, wide), BF16),
            vmem((nz, share, 128), F32),
            vmem((nz, share, 128), BF16),
            vmem((nz, share, 128), BF16),
            vmem((n_space, share, 128), BF16),
            dma((5,)),
            dma((2,)), dma((2,)),
            dma((n_dp,)), dma((n_dp,)), dma((n_dp,)), dma((n_dp,)),
            dma((2,)), dma((2,)),
            dma((n_dp,)), dma((n_dp,)),
            dma((nz,)), dma((nz,)),
            dma((n_space,)), dma((n_space,)),
        ],
        compiler_params=pltpu.CompilerParams(
            collective_id=0, has_side_effects=True, vmem_limit_bytes=24 * 1024 * 1024
        ),
    )(*(pltpu.with_memory_space_constraint(x, pltpu.HBM)
        for x in (image, cotangent, weight_t, moment_one.T, moment_two.T)))
    out, grad_image, new_weight, new_one, new_two = pl.pallas_call(
        functools.partial(finish, count),
        out_shape=(
            jax.ShapeDtypeStruct(cotangent.shape, BF16),
            jax.ShapeDtypeStruct(image.shape, BF16),
            state, state, state,
        ),
        in_specs=[spec] * 6,
        out_specs=[hbm] * 5,
        scratch_shapes=[vmem(weight_t.shape, F32)] * 3 + [dma((5,))],
        compiler_params=pltpu.CompilerParams(vmem_limit_bytes=16 * 1024 * 1024),
    )(out, grad_image, gradient, *held)
    return out, grad_image, new_weight.T, new_one.T, new_two.T


def solution(mesh):
    whole = P("dp", "space", None)
    rows = P("dp", None)
    specs = (whole, whole, rows, rows, rows)
    return jax.shard_map(
        functools.partial(body, mesh.shape["dp"], mesh.shape["space"]),
        mesh=mesh, in_specs=specs, out_specs=specs, check_vma=False)
```
